512 devices in a mesh: rows: 64 (over z_hi, y, x, core), slab: 8 (over z_lo).
Axes of the slice: x: 4, y: 4, z: 16 (z_hi: 2, z_lo: 8; z = z_hi * 8 + z_lo), core: 2. Of those that a mesh axis runs over, the one named last changes fastest.
Arguments:
- prior_vectors: float32 [458752, 384], P(('rows', 'slab'))
- raw_columns: float32 [2, 458752, 256], P(None, ('rows', 'slab')), as said below
- pivot_rows: int32 [2, 256], replicated, may hold values from 0 to 458751, as said below
Outputs:
- new_vectors: float32 [2, 458752, 256], P(None, ('rows', 'slab'))
The draws below stay inside these ranges and needn't reach their ends.
Inputs may be any that keep to these rules, and one draw needn't show every extreme that they name: `pivot_rows`: all 512 entries are distinct pair rows. `raw_columns`: in every step the matrix symmetric of the steps is positive definite.
All inputs are finite; a program needn't handle non-finite values.
Results may differ from the reference program's by a relative error of at most 0.0001.
Values sent between devices are 32-bit elements; how exact they have to be, the bound alone decides.
No kernel may reach another device: no remote copies, remote signals or barrier semaphores. Data moves between devices by JAX's collectives and lax.ppermute only.
A program may use at most 64 MiB of HBM per device.

```python
import jax
import jax.numpy as jnp
from jax import lax

R_DEV = 896
PRIOR = 384
PIV = 256
STEPS = 2
PAIRS = 458752


def shared_draw(key, row_spread, diag_low, diag_high):
    highest = lax.Precision.HIGHEST
    keys = jax.random.split(key, 12)
    device_count = PAIRS // R_DEV
    weighting = jax.random.randint(keys[0], (device_count,), 0, 4)
    indices = jnp.arange(PAIRS, dtype=jnp.int32)
    owner = indices // R_DEV
    level = jax.random.randint(keys[1], (PAIRS,), 0, 512)
    score = (weighting[owner] * 512 + level) * PAIRS + indices
    forced = jnp.logical_or(indices == 0, indices == PAIRS - 1)
    score = jnp.where(forced, 2048 * PAIRS + indices, score)
    picked = lax.top_k(score, STEPS * PIV)[1]
    chosen_all = picked.astype(jnp.int32).reshape(STEPS, PIV)
    prior = jnp.clip(0.3 * jax.random.normal(keys[2], (PAIRS, PRIOR), jnp.float32), -1.2, 1.2)
    vectors = prior
    columns = []
    bound = 0.9 * jnp.sqrt(1.0 * PIV * diag_low) / PIV
    below = jnp.tril(jnp.ones((PIV, PIV), jnp.float32), -1)
    for which_step in range(STEPS):
        chosen = chosen_all[which_step]
        base_keys = jax.random.split(keys[3 + which_step], 4)
        rough = jnp.clip(jax.random.normal(base_keys[0], (PAIRS, PIV), jnp.float32), -3.0, 3.0)
        row_scale = jnp.exp(jax.random.uniform(base_keys[1], (PAIRS, 1), jnp.float32, -0.5, 0.5) * jnp.log(row_spread))
        fresh_vec = 0.5 * rough * row_scale
        off_part = jax.random.uniform(base_keys[2], (PIV, PIV), jnp.float32, -1.0, 1.0) * bound * below
        diag_part = jnp.sqrt(jnp.exp(jax.random.uniform(base_keys[3], (PIV,), jnp.float32, jnp.log(diag_low), jnp.log(diag_high))) * PIV)
        lower_part = off_part + jnp.diag(diag_part)
        fresh_vec = fresh_vec.at[chosen].set(lower_part)
        pivot_vec = jnp.take(vectors, chosen, axis=0)
        columns.append(jnp.dot(fresh_vec, lower_part.T, precision=highest) + jnp.dot(vectors, pivot_vec.T, precision=highest))
        vectors = jnp.concatenate([vectors, fresh_vec], axis=1)
    return (chosen_all, prior, jnp.stack(columns))


def draw_pivot_rows(key, part):
    return shared_draw(key, 1.0, 1.2, 2.4)[0]


def draw_prior_vectors(key, part):
    return shared_draw(key, 1.0, 1.2, 2.4)[1]


def draw_raw_columns(key, part):
    return shared_draw(key, 1.0, 1.2, 2.4)[2]


def setup_inputs(seed: int = 0) -> dict:
    seeds = jax.random.split(jax.random.key(seed), 4)
    prior_vectors = draw_prior_vectors(jax.random.fold_in(seeds[3], 71), 0)
    raw_columns = draw_raw_columns(jax.random.fold_in(seeds[3], 71), 0)
    pivot_rows = draw_pivot_rows(jax.random.fold_in(seeds[3], 71), 0)
    return {"prior_vectors": prior_vectors, "raw_columns": raw_columns, "pivot_rows": pivot_rows}


def reference(prior_vectors, raw_columns, pivot_rows):
    highest = lax.Precision.HIGHEST
    vectors = prior_vectors
    outputs = []
    for which_step in range(STEPS):
        chosen = pivot_rows[which_step].astype(jnp.int32)
        pivot_vec = jnp.take(vectors, chosen, axis=0)
        residual = raw_columns[which_step] - jnp.dot(vectors, pivot_vec.T, precision=highest)
        pivot_block = jnp.take(residual, chosen, axis=0)
        symmetric = 0.5 * (pivot_block + pivot_block.T)
        factor = jnp.linalg.cholesky(symmetric)
        identity = jnp.eye(PIV, dtype=jnp.float32)
        inverse = lax.linalg.triangular_solve(factor, identity, left_side=True, lower=True)
        fresh_vec = jnp.dot(residual, inverse.T, precision=highest)
        outputs.append(fresh_vec)
        vectors = jnp.concatenate([vectors, fresh_vec], axis=1)
    return jnp.stack(outputs)
```

```python
import functools

import jax
import jax.numpy as jnp
from jax import lax
from jax.experimental import pallas as pl
from jax.experimental.pallas import tpu as pltpu
from jax.sharding import Mesh
from jax.sharding import PartitionSpec as P

F32 = jnp.float32
HIGHEST = lax.Precision.HIGHEST
AXES = ("z_hi", "y", "x", "core", "z_lo")
TILE = (8, 128)
VMEM_LIMIT = 48 * 1024 * 1024


def dot(left, right, left_dim=1, right_dim=0):
    dims = (((left_dim,), (right_dim,)), ((), ()))
    return lax.dot_general(left, right, dims, precision=HIGHEST, preferred_element_type=F32)


def pack_kernel(pivots, place, prior, raw, keep, send):
    keep[...] = jnp.zeros_like(keep)
    send[...] = jnp.zeros_like(send)
    offset, core = place[0], place[1]
    rows_here = prior.shape[0]
    groups = keep.shape[0]
    half = groups * 8

    for step in range(2):
        base = 5 * step

        def look(pivot, step=step, base=base):
            row = pivots[step, pivot] - offset
            here = jnp.logical_and(row >= 0, row < rows_here)

            @pl.when(here)
            def _():
                side = pivot // half
                group = lax.rem(pivot, half) // 8
                line = pl.ds(lax.rem(pivot, 8), 1)

                def put(target):
                    values = prior[pl.ds(row, 1), :]
                    for t in range(3):
                        target[group, base + t, line, :] = values[:, 128 * t : 128 * t + 128]
                    for which in range(step + 1):
                        values = raw[which, pl.ds(row, 1), :]
                        for t in range(2):
                            target[group, base + 3 + 2 * which + t, line, :] = values[:, 128 * t : 128 * t + 128]

                @pl.when(side == core)
                def _():
                    put(keep)

                @pl.when(side != core)
                def _():
                    put(send)

        def chunk(which, _):
            for k in range(8):
                look(which * 8 + k)
            return 0

        lax.fori_loop(0, pivots.shape[1] // 8, chunk, 0)


def pack(pivot_rows, place, prior, raw, groups):
    shape = jax.ShapeDtypeStruct((groups, 12) + TILE, F32)
    vmem, smem = pl.BlockSpec(memory_space=pltpu.VMEM), pl.BlockSpec(memory_space=pltpu.SMEM)
    return pl.pallas_call(
        pack_kernel,
        out_shape=(shape, shape),
        in_specs=[smem, smem, vmem, vmem],
        out_specs=(vmem, vmem),
        compiler_params=pltpu.CompilerParams(vmem_limit_bytes=VMEM_LIMIT),
    )(pivot_rows, place, prior, raw)


def eliminate(block, panel):
    width = block.shape[0]
    lanes = 2 * width
    row_of = lax.broadcasted_iota(jnp.int32, (width, width), 0)
    column_of = lax.broadcasted_iota(jnp.int32, (width, width), 1)
    work = jnp.concatenate([block, (row_of == column_of).astype(F32)], axis=1)
    done = []
    for first in range(0, width, panel):
        left = width - first
        columns = [jnp.broadcast_to(work[:, first + k : first + k + 1], (left, lanes)) for k in range(panel)]
        rows, scaled = [], []
        for k in range(panel):
            pivot = jnp.broadcast_to(columns[k][k : k + 1], TILE)
            root = lax.rsqrt(pivot)
            root = (root * (1.5 - 0.5 * pivot * root * root))[0:1]
            row = work[k : k + 1]
            for before in range(k):
                row = row - scaled[before][k : k + 1] * rows[before]
            rows.append(row * root)
            scaled.append(columns[k] * root)
            for after in range(k + 1, panel):
                columns[after] = columns[after] - scaled[k] * (columns[after][k : k + 1] * root)
        done.extend(rows)
        if left > panel:
            work = work[panel:]
            for k in range(panel):
                work = work - scaled[k][panel:] * rows[k]
    return jnp.concatenate(done, axis=0)[:, width:]


def cholesky_inverse(symmetric, width=64, panel=16):
    size = symmetric.shape[0]
    work = symmetric
    finished = []
    for which in range(size // width):
        low = which * width
        rest = size - low - width
        line = work[:width]
        inverse = eliminate(line[:, low : low + width], panel)
        parts = [inverse]
        if low:
            parts.insert(0, jnp.zeros((width, low), F32))
        if rest:
            parts.append(jnp.zeros((width, rest), F32))
        block_of = lax.broadcasted_iota(jnp.int32, (width, size), 1) // width
        line = jnp.where(block_of == which, jnp.concatenate(parts, axis=1), dot(inverse, line))
        finished.append(jnp.where(block_of <= which, line, 0.0))
        if rest:
            block_of = lax.broadcasted_iota(jnp.int32, (rest, size), 1) // width
            work = jnp.where(block_of == which, 0.0, work[width:]) - dot(line[:, low + width :], line, 0, 0)
    return jnp.concatenate(finished, axis=0)


def steps_kernel(place, mine, other, prior, raw, out, packed):
    core = place[1]
    half = mine.shape[0]
    packed[pl.ds(core * half, half)] = mine[...]
    packed[pl.ds((1 - core) * half, half)] = other[...]

    def columns(first, count):
        tiles = [packed[:, first + t].reshape(2 * half * 8, 128) for t in range(count)]
        return jnp.concatenate(tiles, axis=1)

    prior_0, prior_1 = columns(0, 3), columns(5, 3)
    vectors = prior[...]

    def symmetrized(block):
        return 0.5 * (block + block.T)

    inverse_0 = cholesky_inverse(symmetrized(columns(3, 2) - dot(prior_0, prior_0, 1, 1)))
    fresh_pivots = dot(columns(8, 2) - dot(prior_1, prior_0, 1, 1), inverse_0, 1, 1)
    block_1 = columns(10, 2) - dot(prior_1, prior_1, 1, 1) - dot(fresh_pivots, fresh_pivots, 1, 1)
    inverse_1 = cholesky_inverse(symmetrized(block_1))
    fresh = dot(raw[0] - dot(vectors, prior_0, 1, 1), inverse_0, 1, 1)
    out[0] = fresh
    residual = raw[1] - dot(vectors, prior_1, 1, 1) - dot(fresh, fresh_pivots, 1, 1)
    out[1] = dot(residual, inverse_1, 1, 1)


def steps(place, mine, other, prior, raw):
    vmem, smem = pl.BlockSpec(memory_space=pltpu.VMEM), pl.BlockSpec(memory_space=pltpu.SMEM)
    groups = mine.shape[0]
    return pl.pallas_call(
        steps_kernel,
        out_shape=jax.ShapeDtypeStruct(raw.shape, F32),
        in_specs=[smem, vmem, vmem, vmem, vmem],
        out_specs=vmem,
        scratch_shapes=[pltpu.VMEM((2 * groups, 12) + TILE, F32)],
        compiler_params=pltpu.CompilerParams(vmem_limit_bytes=VMEM_LIMIT),
    )(place, mine, other, prior, raw)


def body(prior, raw, pivot_rows):
    rows_here = prior.shape[0]
    core = lax.axis_index("core")
    place = jnp.stack([lax.axis_index(AXES) * rows_here, core]).astype(jnp.int32)
    plane, line = ("y", "x"), ("z_hi", "z_lo")
    in_plane, in_line = lax.axis_size(plane), lax.axis_size(line)
    swap = [(0, 1), (1, 0)]

    keep, send = pack(pivot_rows, place, prior, raw, in_plane)
    total = keep + lax.ppermute(send, "core", swap)
    total = jnp.sum(lax.all_to_all(total, plane, 0, 0), axis=0)
    tiles = total.shape[0]
    total = jnp.concatenate([total, jnp.zeros((in_line - tiles,) + TILE, F32)], axis=0)
    total = jnp.sum(lax.all_to_all(total, line, 0, 0), axis=0)
    total = lax.all_to_all(jnp.broadcast_to(total, (in_line,) + TILE), line, 0, 0)[:tiles]
    mine = lax.all_to_all(jnp.broadcast_to(total, (in_plane,) + total.shape), plane, 0, 0)
    other = lax.ppermute(mine, "core", swap)
    return steps(place, mine, other, prior, raw)


def solution(mesh):
    fine = Mesh(mesh.devices.reshape(2, 4, 4, 2, 8), AXES)
    return jax.shard_map(
        body,
        mesh=fine,
        in_specs=(P(AXES, None), P(None, AXES, None), P()),
        out_specs=P(None, AXES, None),
        check_vma=False,
    )
```

```python
import functools

import jax
import jax.numpy as jnp
from jax import lax
from jax.experimental import pallas as pl
from jax.experimental.pallas import tpu as pltpu
from jax.sharding import Mesh
from jax.sharding import PartitionSpec as P

F32 = jnp.float32
HIGHEST = lax.Precision.HIGHEST
AXES = ("z_hi", "y", "x", "core", "z_lo")
TILE = (8, 128)
VMEM_LIMIT = 48 * 1024 * 1024
PACK_VMEM_LIMIT = 60 * 1024 * 1024


def dot(left, right, left_dim=1, right_dim=0):
    dims = (((left_dim,), (right_dim,)), ((), ()))
    return lax.dot_general(left, right, dims, precision=HIGHEST, preferred_element_type=F32)


def pack_kernel(pivots, place, prior, raw, keep, send, counts, sem):
    keep[...] = jnp.zeros_like(keep)
    send[...] = jnp.zeros_like(send)
    offset, core = place[0], place[1]
    rows_here = jnp.uint32(prior.shape[0])
    per_step = pivots.shape[1]
    chunk = 8

    def local(step, pivot):
        row = pivots[step, pivot] - offset
        return row, row.astype(jnp.uint32) < rows_here

    def tiles(step):
        base = 5 * step
        for t in range(3):
            yield base + t, prior, 128 * t
        for which in range(step + 1):
            for t in range(2):
                yield base + 3 + 2 * which + t, raw.at[which], 128 * t

    def copy(source, row, column, target):
        return pltpu.make_async_copy(source.at[pl.ds(row, 1), pl.ds(column, 128)], target, sem)

    def start(step, pivot):
        row, here = local(step, pivot)

        @pl.when(here)
        def _():
            counts[step] += 1
            half = keep.shape[0]
            group, line = pivot // 8, pl.ds(lax.rem(pivot, 8), 1)
            for side, target in ((core, keep), (1 - core, send)):

                @pl.when(group // half == side)
                def _():
                    for number, source, column in tiles(step):
                        copy(source, row, column, target.at[lax.rem(group, half), number, line]).start()

    for step in range(2):
        counts[step] = 0

        for first in range(0, per_step, chunk):
            found = local(step, first)[1]
            for k in range(1, chunk):
                found = jnp.logical_or(found, local(step, first + k)[1])

            @pl.when(found)
            def _(step=step, first=first):
                lax.fori_loop(0, chunk, lambda k, _: start(step, first + k), None)

    for step in range(2):

        def finish(_, carry, step=step):
            for _, source, column in tiles(step):
                copy(source, 0, column, keep.at[0, 0, pl.ds(0, 1)]).wait()
            return carry

        lax.fori_loop(0, counts[step], finish, 0)


def pack(pivot_rows, place, prior, raw, groups):
    shape = jax.ShapeDtypeStruct((groups, 12) + TILE, F32)
    vmem, smem = pl.BlockSpec(memory_space=pltpu.VMEM), pl.BlockSpec(memory_space=pltpu.SMEM)
    where_it_is = pl.BlockSpec(memory_space=pl.ANY)
    return pl.pallas_call(
        pack_kernel,
        out_shape=(shape, shape),
        in_specs=[smem, smem, where_it_is, where_it_is],
        out_specs=(vmem, vmem),
        scratch_shapes=[pltpu.SMEM((2,), jnp.int32), pltpu.SemaphoreType.DMA],
        compiler_params=pltpu.CompilerParams(vmem_limit_bytes=PACK_VMEM_LIMIT),
    )(pivot_rows, place, prior, raw)


def eliminate(block, panel, beside):
    width = block.shape[0]
    lanes = 2 * width
    row_of = lax.broadcasted_iota(jnp.int32, (width, width), 0)
    column_of = lax.broadcasted_iota(jnp.int32, (width, width), 1)
    work = jnp.concatenate([block, (row_of == column_of).astype(F32)], axis=1)
    done = []
    for first in range(0, width, panel):
        left = width - first
        columns = [jnp.broadcast_to(work[:, first + k : first + k + 1], (left, lanes)) for k in range(panel)]
        rows, scaled = [], []
        for k in range(panel):
            pivot = jnp.broadcast_to(columns[k][k : k + 1], TILE)
            root = lax.rsqrt(pivot)[0:1]
            row = work[k : k + 1]
            for before in range(k):
                row = row - scaled[before][k : k + 1] * rows[before]
            rows.append(row * root)
            scaled.append(columns[k] * root)
            for after in range(k + 1, panel):
                columns[after] = columns[after] - scaled[k] * (columns[after][k : k + 1] * root)
        done.extend(rows)
        beside()
        if left > panel:
            work = work[panel:]
            for k in range(panel):
                work = work - scaled[k][panel:] * rows[k]
    return jnp.concatenate(done, axis=0)[:, width:]


def cholesky_inverse(symmetric, beside, width=64, panel=16):
    size = symmetric.shape[0]
    work = symmetric
    finished = []
    for which in range(size // width):
        low = which * width
        rest = size - low - width
        line = work[:width]
        inverse = eliminate(line[:, low : low + width], panel, beside)
        parts = [inverse]
        if low:
            parts.insert(0, jnp.zeros((width, low), F32))
        if rest:
            parts.append(jnp.zeros((width, rest), F32))
        block_of = lax.broadcasted_iota(jnp.int32, (width, size), 1) // width
        line = jnp.where(block_of == which, jnp.concatenate(parts, axis=1), dot(inverse, line))
        finished.append(jnp.where(block_of <= which, line, 0.0))
        if rest:
            block_of = lax.broadcasted_iota(jnp.int32, (rest, size), 1) // width
            work = jnp.where(block_of == which, 0.0, work[width:]) - dot(line[:, low + width :], line, 0, 0)
    return jnp.concatenate(finished, axis=0)


def steps_kernel(place, mine, other, prior, raw, out, packed):
    core = place[1]
    half = mine.shape[0]
    packed[pl.ds(core * half, half)] = mine[...]
    packed[pl.ds((1 - core) * half, half)] = other[...]

    def columns(first, count):
        tiles = [packed[:, first + t].reshape(2 * half * 8, 128) for t in range(count)]
        return jnp.concatenate(tiles, axis=1)

    prior_0, prior_1 = columns(0, 3), columns(5, 3)
    rows_here = prior.shape[0]
    chunks = [slice(rows_here * c // 4, rows_here * (c + 1) // 4) for c in range(4)]

    def symmetrized(block):
        return 0.5 * (block + block.T)

    def residual(step, pivots, rows):
        out[step, rows] = raw[step, rows] - dot(prior[rows], pivots, 1, 1)

    def finish(step, inverse, rows):
        out[step, rows] = dot(out[step, rows], inverse, 1, 1)

    def take(pivots, rows):
        out[1, rows] = out[1, rows] - dot(out[0, rows], pivots, 1, 1)

    def beside(tasks):
        calls = iter(range(1000))

        def call():
            if next(calls) % 2 == 0 and tasks:
                tasks.pop(0)()

        return call

    tasks = [functools.partial(residual, 0, prior_0, rows) for rows in chunks]
    tasks += [functools.partial(residual, 1, prior_1, rows) for rows in chunks]
    inverse_0 = cholesky_inverse(symmetrized(columns(3, 2) - dot(prior_0, prior_0, 1, 1)), beside(tasks))
    fresh_pivots = dot(columns(8, 2) - dot(prior_1, prior_0, 1, 1), inverse_0, 1, 1)
    block_1 = columns(10, 2) - dot(prior_1, prior_1, 1, 1) - dot(fresh_pivots, fresh_pivots, 1, 1)
    tasks += [functools.partial(finish, 0, inverse_0, rows) for rows in chunks]
    tasks += [functools.partial(take, fresh_pivots, rows) for rows in chunks]
    inverse_1 = cholesky_inverse(symmetrized(block_1), beside(tasks))
    for task in tasks:
        task()
    for rows in chunks:
        finish(1, inverse_1, rows)


def steps(place, mine, other, prior, raw):
    vmem, smem = pl.BlockSpec(memory_space=pltpu.VMEM), pl.BlockSpec(memory_space=pltpu.SMEM)
    groups = mine.shape[0]
    return pl.pallas_call(
        steps_kernel,
        out_shape=jax.ShapeDtypeStruct(raw.shape, F32),
        in_specs=[smem, vmem, vmem, vmem, vmem],
        out_specs=vmem,
        scratch_shapes=[pltpu.VMEM((2 * groups, 12) + TILE, F32)],
        compiler_params=pltpu.CompilerParams(vmem_limit_bytes=VMEM_LIMIT),
    )(place, mine, other, prior, raw)


def body(prior, raw, pivot_rows):
    rows_here = prior.shape[0]
    core = lax.axis_index("core")
    place = jnp.stack([lax.axis_index(AXES) * rows_here, core]).astype(jnp.int32)
    plane, line = ("y", "x"), ("z_hi", "z_lo")
    in_plane, in_line = lax.axis_size(plane), lax.axis_size(line)
    swap = [(0, 1), (1, 0)]

    keep, send = pack(pivot_rows, place, prior, raw, in_plane)
    total = keep + lax.ppermute(send, "core", swap)
    total = jnp.sum(lax.all_to_all(total, plane, 0, 0), axis=0)
    tiles = total.shape[0]
    total = jnp.concatenate([total, jnp.zeros((in_line - tiles,) + TILE, F32)], axis=0)
    total = jnp.sum(lax.all_to_all(total, line, 0, 0), axis=0)
    total = lax.all_to_all(jnp.broadcast_to(total, (in_line,) + TILE), line, 0, 0)[:tiles]
    mine = lax.all_to_all(jnp.broadcast_to(total, (in_plane,) + total.shape), plane, 0, 0)
    other = lax.ppermute(mine, "core", swap)
    return steps(place, mine, other, prior, raw)


def solution(mesh):
    fine = Mesh(mesh.devices.reshape(2, 4, 4, 2, 8), AXES)
    return jax.shard_map(
        body,
        mesh=fine,
        in_specs=(P(AXES, None), P(None, AXES, None), P()),
        out_specs=P(None, AXES, None),
        check_vma=False,
    )
```

```python
import functools

import jax
import jax.numpy as jnp
from jax import lax
from jax.experimental import pallas as pl
from jax.experimental.pallas import tpu as pltpu
from jax.sharding import Mesh
from jax.sharding import PartitionSpec as P

F32 = jnp.float32
HIGHEST = lax.Precision.HIGHEST
AXES = ("z_hi", "y", "x", "core", "z_lo")
TILE = (8, 128)
VMEM_LIMIT = 48 * 1024 * 1024
PACK_VMEM_LIMIT = 60 * 1024 * 1024


def dot(left, right, left_dim=1, right_dim=0):
    dims = (((left_dim,), (right_dim,)), ((), ()))
    return lax.dot_general(left, right, dims, precision=HIGHEST, preferred_element_type=F32)


def pack_kernel(pivots, prior, raw, keep, send, counts, sem):
    keep[...] = jnp.zeros_like(keep)
    send[...] = jnp.zeros_like(send)
    rows_here = prior.shape[0]
    offset, core = lax.axis_index(AXES) * rows_here, lax.axis_index("core")
    per_step = pivots.shape[1]
    chunk = 8

    def local(step, pivot):
        row = pivots[step, pivot] - offset
        return row, row.astype(jnp.uint32) < jnp.uint32(rows_here)

    def tiles(step):
        base = 5 * step
        for t in range(3):
            yield base + t, prior, 128 * t
        for which in range(step + 1):
            for t in range(2):
                yield base + 3 + 2 * which + t, raw.at[which], 128 * t

    def copy(source, row, column, target):
        return pltpu.make_async_copy(source.at[pl.ds(row, 1), pl.ds(column, 128)], target, sem)

    def start(step, pivot):
        row, here = local(step, pivot)

        @pl.when(here)
        def _():
            counts[step] += 1
            half = keep.shape[0]
            group, line = pivot // 8, pl.ds(lax.rem(pivot, 8), 1)
            for side, target in ((core, keep), (1 - core, send)):

                @pl.when(group // half == side)
                def _():
                    for number, source, column in tiles(step):
                        copy(source, row, column, target.at[lax.rem(group, half), number, line]).start()

    for step in range(2):
        counts[step] = 0

        for first in range(0, per_step, chunk):
            found = local(step, first)[1]
            for k in range(1, chunk):
                found = jnp.logical_or(found, local(step, first + k)[1])

            @pl.when(found)
            def _(step=step, first=first):
                lax.fori_loop(0, chunk, lambda k, _: start(step, first + k), None)

    for step in range(2):

        def finish(_, carry, step=step):
            for _, source, column in tiles(step):
                copy(source, 0, column, keep.at[0, 0, pl.ds(0, 1)]).wait()
            return carry

        lax.fori_loop(0, counts[step], finish, 0)


def pack(pivot_rows, prior, raw, groups):
    shape = jax.ShapeDtypeStruct((groups, 12) + TILE, F32)
    vmem, smem = pl.BlockSpec(memory_space=pltpu.VMEM), pl.BlockSpec(memory_space=pltpu.SMEM)
    where_it_is = pl.BlockSpec(memory_space=pl.ANY)
    return pl.pallas_call(
        pack_kernel,
        out_shape=(shape, shape),
        in_specs=[smem, where_it_is, where_it_is],
        out_specs=(vmem, vmem),
        scratch_shapes=[pltpu.SMEM((2,), jnp.int32), pltpu.SemaphoreType.DMA],
        compiler_params=pltpu.CompilerParams(vmem_limit_bytes=PACK_VMEM_LIMIT),
    )(pivot_rows, prior, raw)


def spread(line):
    return jnp.broadcast_to(line, TILE)


def eliminate(block, at, beside):
    width = block.shape[0]
    row_of = lax.broadcasted_iota(jnp.int32, (width, width), 0)
    column_of = lax.broadcasted_iota(jnp.int32, (width, width), 1)
    line_of = lax.broadcasted_iota(jnp.int32, TILE, 0)
    halves = [block, (row_of == column_of).astype(F32)]
    work = jnp.concatenate(halves[:: -1 if at else 1], axis=1)
    done = []
    columns = [jnp.broadcast_to(work[:8, at + k : at + k + 1], TILE) for k in range(8)]
    for first in range(0, width, 8):
        left = width - first
        below = left // 8 - 1
        head, finished, rows, under, after = work[:8], work[:8], [], [], []
        if below:
            for k in range(8, 16):
                after.append(jnp.broadcast_to(work[8:16, at + first + k : at + first + k + 1], TILE))
            for k in range(8):
                column = jnp.broadcast_to(work[8:, at + first + k : at + first + k + 1], (left - 8, 128))
                under.append(column.reshape((below,) + TILE))
        for k in range(8):
            root = lax.rsqrt(spread(columns[k][k : k + 1]))
            scaled = columns[k] * root
            rows.append(spread(head[k : k + 1]) * root)
            finished = jnp.where(line_of == k, rows[k], finished)
            if k < 7:
                head = head - scaled * rows[k]
            if below:
                under[k] = under[k] * root
            for m in range(k + 1, 8):
                factor = spread(scaled[m : m + 1])
                columns[m] = columns[m] - scaled * factor
                if below:
                    under[m] = under[m] - under[k] * factor
        done.append(finished)
        if below:
            for k in range(8):
                column = under[k][0]
                for m in range(8):
                    after[m] = after[m] - column * spread(column[m : m + 1])
            columns = after
            work = work[8:].reshape((below,) + TILE)
            for k in range(8):
                work = work - under[k] * rows[k]
            work = work.reshape(left - 8, 128)
        beside()
    return jnp.concatenate(done, axis=0)


def cholesky_inverse(symmetric, beside):
    size, width = symmetric.shape[0], 64
    work = symmetric
    finished = []
    for which in range(size // width):
        low, high = which * width, (which + 1) * width
        at = low % 128
        rest = size - high
        block_of = lax.broadcasted_iota(jnp.int32, (width, size), 1) // width
        on_diagonal = lax.broadcasted_iota(jnp.int32, (width, size), 1) == lax.broadcasted_iota(jnp.int32, (width, size), 0) + low
        line = jnp.where(block_of == which, on_diagonal.astype(F32), work[:width])
        blank = jnp.zeros_like(line)
        line = jnp.concatenate([blank, line] if at == 0 else [line, blank], axis=0)
        inverse = eliminate(work[:width, low:high], at, beside)
        if rest:
            column = work[width:, low:high]
            blank = jnp.zeros_like(column)
            column = jnp.concatenate([blank, column] if at == 0 else [column, blank], axis=1)
            factor = dot(column, inverse, 1, 1)
            block_of_rest = lax.broadcasted_iota(jnp.int32, (rest, size), 1) // width
            work = jnp.where(block_of_rest == which, 0.0, work[width:])
        line = dot(inverse, line)
        if rest:
            work = work - dot(factor, line)
        finished.append(jnp.where(block_of <= which, line, 0.0))
    return jnp.concatenate(finished, axis=0)


def steps_kernel(mine, other, prior, raw, out, packed):
    core = lax.axis_index("core")
    half = mine.shape[0]
    packed[pl.ds(core * half, half)] = mine[...]
    packed[pl.ds((1 - core) * half, half)] = other[...]

    def columns(first, count):
        tiles = [packed[:, first + t].reshape(2 * half * 8, 128) for t in range(count)]
        return jnp.concatenate(tiles, axis=1)

    prior_0, prior_1 = columns(0, 3), columns(5, 3)
    rows_here = prior.shape[0]
    chunks = [slice(rows_here * c // 4, rows_here * (c + 1) // 4) for c in range(4)]

    def symmetrized(block):
        return 0.5 * (block + block.T)

    def residual(step, pivots, rows):
        out[step, rows] = raw[step, rows] - dot(prior[rows], pivots, 1, 1)

    def finish(step, inverse, rows):
        out[step, rows] = dot(out[step, rows], inverse, 1, 1)

    def take(pivots, rows):
        out[1, rows] = out[1, rows] - dot(out[0, rows], pivots, 1, 1)

    def beside(tasks):
        calls = iter(range(1000))

        def call():
            if next(calls) % 3 == 0 and tasks:
                tasks.pop(0)()

        return call

    tasks = [functools.partial(residual, 0, prior_0, rows) for rows in chunks]
    tasks += [functools.partial(residual, 1, prior_1, rows) for rows in chunks]
    later = {}

    def cross():
        later["cross"] = columns(8, 2) - dot(prior_1, prior_0, 1, 1)

    def block():
        later["block"] = symmetrized(columns(10, 2) - dot(prior_1, prior_1, 1, 1))

    tasks.insert(0, cross)
    tasks.insert(0, block)
    inverse_0 = cholesky_inverse(symmetrized(columns(3, 2) - dot(prior_0, prior_0, 1, 1)), beside(tasks))
    fresh_pivots = dot(later["cross"], inverse_0, 1, 1)
    block_1 = later["block"] - symmetrized(dot(fresh_pivots, fresh_pivots, 1, 1))
    tasks += [functools.partial(finish, 0, inverse_0, rows) for rows in chunks]
    tasks += [functools.partial(take, fresh_pivots, rows) for rows in chunks]
    inverse_1 = cholesky_inverse(block_1, beside(tasks))
    for task in tasks:
        task()
    for rows in chunks:
        finish(1, inverse_1, rows)


def steps(mine, other, prior, raw):
    vmem = pl.BlockSpec(memory_space=pltpu.VMEM)
    groups = mine.shape[0]
    return pl.pallas_call(
        steps_kernel,
        out_shape=jax.ShapeDtypeStruct(raw.shape, F32),
        in_specs=[vmem] * 4,
        out_specs=vmem,
        scratch_shapes=[pltpu.VMEM((2 * groups, 12) + TILE, F32)],
        compiler_params=pltpu.CompilerParams(vmem_limit_bytes=VMEM_LIMIT),
    )(mine, other, prior, raw)


def body(prior, raw, pivot_rows):
    plane, line = ("y", "x"), ("z_hi", "z_lo")
    in_plane = lax.axis_size(plane)
    swap = [(0, 1), (1, 0)]

    keep, send = pack(pivot_rows, prior, raw, in_plane)
    total = keep + lax.ppermute(send, "core", swap)
    total = jnp.sum(lax.all_to_all(total, plane, 0, 0), axis=0)
    for groups in ([[4 * run + k for k in range(4)] for run in range(4)], [[4 * run + k for run in range(4)] for k in range(4)]):
        copies = jnp.broadcast_to(total, (4,) + total.shape)
        total = jnp.sum(lax.all_to_all(copies, line, 0, 0, axis_index_groups=groups), axis=0)
    mine = lax.all_to_all(jnp.broadcast_to(total, (in_plane,) + total.shape), plane, 0, 0)
    other = lax.ppermute(mine, "core", swap)
    return steps(mine, other, prior, raw)


def solution(mesh):
    fine = Mesh(mesh.devices.reshape(2, 4, 4, 2, 8), AXES)
    return jax.shard_map(
        body,
        mesh=fine,
        in_specs=(P(AXES, None), P(None, AXES, None), P()),
        out_specs=P(None, AXES, None),
        check_vma=False,
    )
```

```python
import functools

import jax
import jax.numpy as jnp
from jax import lax
from jax.experimental import pallas as pl
from jax.experimental.pallas import tpu as pltpu
from jax.sharding import Mesh
from jax.sharding import PartitionSpec as P

F32 = jnp.float32
HIGHEST = lax.Precision.HIGHEST
AXES = ("z_hi", "y", "x", "core", "z_lo")
TILE = (8, 128)
VMEM_LIMIT = 48 * 1024 * 1024
PACK_VMEM_LIMIT = 56 * 1024 * 1024


def dot(left, right, left_dim=1, right_dim=0):
    dims = (((left_dim,), (right_dim,)), ((), ()))
    return lax.dot_general(left, right, dims, precision=HIGHEST, preferred_element_type=F32)


def pack_kernel(pivots, prior, raw, keep, send, counts, sem):
    keep[...] = jnp.zeros_like(keep)
    send[...] = jnp.zeros_like(send)
    rows_here = prior.shape[0]
    offset, core = lax.axis_index(AXES) * rows_here, lax.axis_index("core")
    per_step = pivots.shape[1]
    chunk = 8

    def local(step, pivot):
        row = pivots[step, pivot] - offset
        return row, row.astype(jnp.uint32) < jnp.uint32(rows_here)

    def tiles(step):
        base = 5 * step
        for t in range(3):
            yield base + t, prior, 128 * t
        for which in range(step + 1):
            for t in range(2):
                yield base + 3 + 2 * which + t, raw.at[which], 128 * t

    def copy(source, row, column, target):
        return pltpu.make_async_copy(source.at[pl.ds(row, 1), pl.ds(column, 128)], target, sem)

    def start(step, pivot):
        row, here = local(step, pivot)

        @pl.when(here)
        def _():
            counts[step] += 1
            half = keep.shape[0]
            group, line = pivot // 8, pl.ds(lax.rem(pivot, 8), 1)
            for side, target in ((core, keep), (1 - core, send)):

                @pl.when(group // half == side)
                def _():
                    for number, source, column in tiles(step):
                        copy(source, row, column, target.at[lax.rem(group, half), number, line]).start()

    for step in range(2):
        counts[step] = 0

        for first in range(0, per_step, chunk):
            found = local(step, first)[1]
            for k in range(1, chunk):
                found = jnp.logical_or(found, local(step, first + k)[1])

            @pl.when(found)
            def _(step=step, first=first):
                lax.fori_loop(0, chunk, lambda k, _: start(step, first + k), None)

    for step in range(2):

        def finish(_, carry, step=step):
            for _, source, column in tiles(step):
                copy(source, 0, column, keep.at[0, 0, pl.ds(0, 1)]).wait()
            return carry

        lax.fori_loop(0, counts[step], finish, 0)


def pack(pivot_rows, prior, raw, groups):
    shape = pltpu.VMEM((groups, 12) + TILE, F32)
    vmem, smem = pl.BlockSpec(memory_space=pltpu.VMEM), pl.BlockSpec(memory_space=pltpu.SMEM)
    where_it_is = pl.BlockSpec(memory_space=pl.ANY)
    return pl.pallas_call(
        pack_kernel,
        out_shape=(shape, shape),
        in_specs=[smem, where_it_is, where_it_is],
        out_specs=(vmem, vmem),
        scratch_shapes=[pltpu.SMEM((2,), jnp.int32), pltpu.SemaphoreType.DMA],
        compiler_params=pltpu.CompilerParams(vmem_limit_bytes=PACK_VMEM_LIMIT),
    )(pivot_rows, prior, raw)


def spread(line):
    return jnp.broadcast_to(line, TILE)


def eliminate(block, at, beside):
    width = block.shape[0]
    row_of = lax.broadcasted_iota(jnp.int32, (width, width), 0)
    column_of = lax.broadcasted_iota(jnp.int32, (width, width), 1)
    line_of = lax.broadcasted_iota(jnp.int32, TILE, 0)
    halves = [block, (row_of == column_of).astype(F32)]
    work = jnp.concatenate(halves[:: -1 if at else 1], axis=1)
    done = []
    columns = [jnp.broadcast_to(work[:8, at + k : at + k + 1], TILE) for k in range(8)]
    for first in range(0, width, 8):
        left = width - first
        below = left // 8 - 1
        head, finished, rows, under, after = work[:8], work[:8], [], [], []
        if below:
            for k in range(8, 16):
                after.append(jnp.broadcast_to(work[8:16, at + first + k : at + first + k + 1], TILE))
            for k in range(8):
                column = jnp.broadcast_to(work[8:, at + first + k : at + first + k + 1], (left - 8, 128))
                under.append(column.reshape((below,) + TILE))
        for k in range(8):
            root = lax.rsqrt(spread(columns[k][k : k + 1]))
            scaled = columns[k] * root
            rows.append(spread(head[k : k + 1]) * root)
            finished = jnp.where(line_of == k, rows[k], finished)
            if k < 7:
                head = head - scaled * rows[k]
            if below:
                under[k] = under[k] * root
            for m in range(k + 1, 8):
                factor = spread(scaled[m : m + 1])
                columns[m] = columns[m] - scaled * factor
                if below:
                    under[m] = under[m] - under[k] * factor
        done.append(finished)
        if below:
            for k in range(8):
                column = under[k][0]
                for m in range(8):
                    after[m] = after[m] - column * spread(column[m : m + 1])
            columns = after
            work = work[8:].reshape((below,) + TILE)
            for k in range(8):
                work = work - under[k] * rows[k]
            work = work.reshape(left - 8, 128)
        beside()
    return jnp.concatenate(done, axis=0)


def cholesky_inverse(symmetric, beside):
    size, width = symmetric.shape[0], 64
    work = symmetric
    finished = []
    for which in range(size // width):
        low, high = which * width, (which + 1) * width
        at = low % 128
        rest = size - high
        block_of = lax.broadcasted_iota(jnp.int32, (width, size), 1) // width
        on_diagonal = lax.broadcasted_iota(jnp.int32, (width, size), 1) == lax.broadcasted_iota(jnp.int32, (width, size), 0) + low
        line = jnp.where(block_of == which, on_diagonal.astype(F32), work[:width])
        blank = jnp.zeros_like(line)
        line = jnp.concatenate([blank, line] if at == 0 else [line, blank], axis=0)
        inverse = eliminate(work[:width, low:high], at, beside)
        if rest:
            column = work[width:, low:high]
            blank = jnp.zeros_like(column)
            column = jnp.concatenate([blank, column] if at == 0 else [column, blank], axis=1)
            factor = dot(column, inverse, 1, 1)
            block_of_rest = lax.broadcasted_iota(jnp.int32, (rest, size), 1) // width
            work = jnp.where(block_of_rest == which, 0.0, work[width:])
        line = dot(inverse, line)
        if rest:
            work = work - dot(factor, line)
        finished.append(jnp.where(block_of <= which, line, 0.0))
    return jnp.concatenate(finished, axis=0)


def steps_kernel(mine, other, prior, raw, result, packed, out, sems):
    core = lax.axis_index("core")
    half = mine.shape[0]
    packed[pl.ds(core * half, half)] = mine[...]
    packed[pl.ds((1 - core) * half, half)] = other[...]

    def columns(first, count):
        tiles = [packed[:, first + t].reshape(2 * half * 8, 128) for t in range(count)]
        return jnp.concatenate(tiles, axis=1)

    prior_0, prior_1 = columns(0, 3), columns(5, 3)
    rows_here = prior.shape[0]
    copies = []
    chunks = [slice(rows_here * c // 4, rows_here * (c + 1) // 4) for c in range(4)]

    def symmetrized(block):
        return 0.5 * (block + block.T)

    def residual(step, pivots, rows):
        out[step, rows] = raw[step, rows] - dot(prior[rows], pivots, 1, 1)

    def finish(step, inverse, rows):
        out[step, rows] = dot(out[step, rows], inverse, 1, 1)
        copies.append(pltpu.make_async_copy(out.at[step, rows], result.at[step, rows], sems.at[len(copies)]))
        copies[-1].start()

    def take(pivots, rows):
        out[1, rows] = out[1, rows] - dot(out[0, rows], pivots, 1, 1)

    def beside(tasks):
        calls = iter(range(1000))

        def call():
            if next(calls) % 3 == 0 and tasks:
                tasks.pop(0)()

        return call

    tasks = [functools.partial(residual, 0, prior_0, rows) for rows in chunks]
    tasks += [functools.partial(residual, 1, prior_1, rows) for rows in chunks]
    later = {}

    def cross():
        later["cross"] = columns(8, 2) - dot(prior_1, prior_0, 1, 1)

    def block():
        later["block"] = symmetrized(columns(10, 2)) - dot(prior_1, prior_1, 1, 1)

    tasks.insert(0, cross)
    tasks.insert(0, block)
    inverse_0 = cholesky_inverse(symmetrized(columns(3, 2)) - dot(prior_0, prior_0, 1, 1), beside(tasks))
    fresh_pivots = dot(later["cross"], inverse_0, 1, 1)
    block_1 = later["block"] - dot(fresh_pivots, fresh_pivots, 1, 1)
    tasks += [functools.partial(finish, 0, inverse_0, rows) for rows in chunks]
    tasks += [functools.partial(take, fresh_pivots, rows) for rows in chunks]
    inverse_1 = cholesky_inverse(block_1, beside(tasks))
    for task in tasks:
        task()
    for rows in chunks:
        finish(1, inverse_1, rows)
    for copy in copies:
        copy.wait()


def steps(mine, other, prior, raw):
    vmem = pl.BlockSpec(memory_space=pltpu.VMEM)
    groups = mine.shape[0]
    return pl.pallas_call(
        steps_kernel,
        out_shape=jax.ShapeDtypeStruct(raw.shape, F32),
        in_specs=[vmem] * 4,
        out_specs=pl.BlockSpec(memory_space=pl.ANY),
        scratch_shapes=[
            pltpu.VMEM((2 * groups, 12) + TILE, F32),
            pltpu.VMEM(raw.shape, F32),
            pltpu.SemaphoreType.DMA((8,)),
        ],
        compiler_params=pltpu.CompilerParams(vmem_limit_bytes=VMEM_LIMIT),
    )(mine, other, prior, raw)


def body(prior, raw, pivot_rows):
    plane, line = ("y", "x"), ("z_hi", "z_lo")
    in_plane = lax.axis_size(plane)
    swap = [(0, 1), (1, 0)]

    keep, send = pack(pivot_rows, prior, raw, in_plane)
    total = keep + lax.ppermute(send, "core", swap)
    total = jnp.sum(lax.all_to_all(total, plane, 0, 0), axis=0)
    for groups in ([[4 * run + k for k in range(4)] for run in range(4)], [[4 * run + k for run in range(4)] for k in range(4)]):
        copies = jnp.broadcast_to(total, (4,) + total.shape)
        total = jnp.sum(lax.all_to_all(copies, line, 0, 0, axis_index_groups=groups), axis=0)
    mine = lax.all_to_all(jnp.broadcast_to(total, (in_plane,) + total.shape), plane, 0, 0)
    other = lax.ppermute(mine, "core", swap)
    return steps(mine, other, prior, raw)


def solution(mesh):
    fine = Mesh(mesh.devices.reshape(2, 4, 4, 2, 8), AXES)
    return jax.shard_map(
        body,
        mesh=fine,
        in_specs=(P(AXES, None), P(None, AXES, None), P()),
        out_specs=P(None, AXES, None),
        check_vma=False,
    )
```

```python
import functools

import jax
import jax.numpy as jnp
from jax import lax
from jax.experimental import pallas as pl
from jax.experimental.pallas import tpu as pltpu
from jax.sharding import Mesh
from jax.sharding import PartitionSpec as P

F32 = jnp.float32
HIGHEST = lax.Precision.HIGHEST
AXES = ("z_hi", "y", "x", "core", "z_lo")
TILE = (8, 128)
VMEM_LIMIT = 48 * 1024 * 1024
PACK_VMEM_LIMIT = 56 * 1024 * 1024


def dot(left, right, left_dim=1, right_dim=0):
    dims = (((left_dim,), (right_dim,)), ((), ()))
    return lax.dot_general(left, right, dims, precision=HIGHEST, preferred_element_type=F32)


def pack_kernel(pivots, prior, raw, keep, send, counts, sem):
    keep[...] = jnp.zeros_like(keep)
    send[...] = jnp.zeros_like(send)
    rows_here = prior.shape[0]
    offset, core = lax.axis_index(AXES) * rows_here, lax.axis_index("core")
    per_step = pivots.shape[1]
    chunk = 8

    def local(step, pivot):
        row = pivots[step, pivot] - offset
        return row, row.astype(jnp.uint32) < jnp.uint32(rows_here)

    def tiles(step):
        base = 5 * step
        for t in range(3):
            yield base + t, prior, 128 * t
        for which in range(step + 1):
            for t in range(2):
                yield base + 3 + 2 * which + t, raw.at[which], 128 * t

    def copy(source, row, column, target):
        return pltpu.make_async_copy(source.at[pl.ds(row, 1), pl.ds(column, 128)], target, sem)

    def start(step, pivot):
        row, here = local(step, pivot)

        @pl.when(here)
        def _():
            counts[step] += 1
            half = keep.shape[0]
            group, line = pivot // 8, pl.ds(lax.rem(pivot, 8), 1)
            for side, target in ((core, keep), (1 - core, send)):

                @pl.when(group // half == side)
                def _():
                    for number, source, column in tiles(step):
                        copy(source, row, column, target.at[lax.rem(group, half), number, line]).start()

    for step in range(2):
        counts[step] = 0

        for first in range(0, per_step, chunk):
            found = local(step, first)[1]
            for k in range(1, chunk):
                found = jnp.logical_or(found, local(step, first + k)[1])

            @pl.when(found)
            def _(step=step, first=first):
                lax.fori_loop(0, chunk, lambda k, _: start(step, first + k), None)

    for step in range(2):

        def finish(_, carry, step=step):
            for _, source, column in tiles(step):
                copy(source, 0, column, keep.at[0, 0, pl.ds(0, 1)]).wait()
            return carry

        lax.fori_loop(0, counts[step], finish, 0)


def pack(pivot_rows, prior, raw, groups):
    shape = pltpu.VMEM((groups, 12) + TILE, F32)
    vmem, smem = pl.BlockSpec(memory_space=pltpu.VMEM), pl.BlockSpec(memory_space=pltpu.SMEM)
    where_it_is = pl.BlockSpec(memory_space=pl.ANY)
    return pl.pallas_call(
        pack_kernel,
        out_shape=(shape, shape),
        in_specs=[smem, where_it_is, where_it_is],
        out_specs=(vmem, vmem),
        scratch_shapes=[pltpu.SMEM((2,), jnp.int32), pltpu.SemaphoreType.DMA],
        compiler_params=pltpu.CompilerParams(vmem_limit_bytes=PACK_VMEM_LIMIT),
    )(pivot_rows, prior, raw)


def spread(line):
    return jnp.broadcast_to(line, TILE)


def eliminate(block, at, beside):
    width = block.shape[0]
    row_of = lax.broadcasted_iota(jnp.int32, (width, width), 0)
    column_of = lax.broadcasted_iota(jnp.int32, (width, width), 1)
    line_of = lax.broadcasted_iota(jnp.int32, TILE, 0)
    halves = [block, (row_of == column_of).astype(F32)]
    work = jnp.concatenate(halves[:: -1 if at else 1], axis=1)
    done = []
    columns = [jnp.broadcast_to(work[:8, at + k : at + k + 1], TILE) for k in range(8)]
    for first in range(0, width, 8):
        left = width - first
        below = left // 8 - 1
        head, finished, rows, under, after = work[:8], work[:8], [], [], []
        if below:
            for k in range(8, 16):
                after.append(jnp.broadcast_to(work[8:16, at + first + k : at + first + k + 1], TILE))
            for k in range(8):
                column = jnp.broadcast_to(work[8:, at + first + k : at + first + k + 1], (left - 8, 128))
                under.append(column.reshape((below,) + TILE))
        for k in range(8):
            root = lax.rsqrt(spread(columns[k][k : k + 1]))
            scaled = columns[k] * root
            rows.append(spread(head[k : k + 1]) * root)
            finished = jnp.where(line_of == k, rows[k], finished)
            if k < 7:
                head = head - scaled * rows[k]
            if below:
                under[k] = under[k] * root
            for m in range(k + 1, 8):
                factor = spread(scaled[m : m + 1])
                columns[m] = columns[m] - scaled * factor
                if below:
                    under[m] = under[m] - under[k] * factor
        done.append(finished)
        if below:
            for k in range(8):
                column = under[k][0]
                for m in range(8):
                    after[m] = after[m] - column * spread(column[m : m + 1])
            columns = after
            work = work[8:].reshape((below,) + TILE)
            for k in range(8):
                work = work - under[k] * rows[k]
            work = work.reshape(left - 8, 128)
        beside()
    return jnp.concatenate(done, axis=0)


def cholesky_inverse(first, whole, beside):
    width, size = first.shape[0], 4 * first.shape[0]
    finished, made = [], []
    for which in range(size // width):
        low, high = which * width, (which + 1) * width
        at = low % 128
        rest = size - high
        urgent = [whole]

        def call(urgent=urgent):
            if urgent:
                made.append(urgent.pop()())
            else:
                beside()

        inverse = eliminate(first, at, call)
        work = made[-1]
        block_of = lax.broadcasted_iota(jnp.int32, (width, size), 1) // width
        on_diagonal = lax.broadcasted_iota(jnp.int32, (width, size), 1) == lax.broadcasted_iota(jnp.int32, (width, size), 0) + low
        line = jnp.where(block_of == which, on_diagonal.astype(F32), work[:width])
        blank = jnp.zeros_like(line)
        line = dot(inverse, jnp.concatenate([blank, line] if at == 0 else [line, blank], axis=0))
        if rest:
            column = work[width:, low:high]
            blank = jnp.zeros_like(column)
            column = jnp.concatenate([blank, column] if at == 0 else [column, blank], axis=1)
            tile = slice(high // 128 * 128, high // 128 * 128 + 128)
            near = work[width : 2 * width, tile] - dot(dot(column[:width], inverse, 1, 1), line[:, tile])
            first = near[:, high % 128 : high % 128 + width]

            def whole(work=work, column=column, inverse=inverse, line=line, which=which, rest=rest):
                block_of = lax.broadcasted_iota(jnp.int32, (rest, size), 1) // width
                return jnp.where(block_of == which, 0.0, work[width:]) - dot(dot(column, inverse, 1, 1), line)

        finished.append(jnp.where(block_of <= which, line, 0.0))
    return jnp.concatenate(finished, axis=0)


def steps_kernel(mine, other, prior, raw, result, packed, out, sems):
    core = lax.axis_index("core")
    half = mine.shape[0]
    packed[pl.ds(core * half, half)] = mine[...]
    packed[pl.ds((1 - core) * half, half)] = other[...]

    def columns(first, count):
        tiles = [packed[:, first + t].reshape(2 * half * 8, 128) for t in range(count)]
        return jnp.concatenate(tiles, axis=1)

    prior_0, prior_1 = columns(0, 3), columns(5, 3)
    rows_here = prior.shape[0]
    copies = []
    chunks = [slice(rows_here * c // 4, rows_here * (c + 1) // 4) for c in range(4)]

    def symmetrized(block):
        return 0.5 * (block + block.T)

    def residual(step, pivots, rows):
        out[step, rows] = raw[step, rows] - dot(prior[rows], pivots, 1, 1)

    def finish(step, inverse, rows):
        out[step, rows] = dot(out[step, rows], inverse, 1, 1)
        copies.append(pltpu.make_async_copy(out.at[step, rows], result.at[step, rows], sems.at[len(copies)]))
        copies[-1].start()

    def take(rows):
        out[1, rows] = out[1, rows] - dot(out[0, rows], later["fresh"], 1, 1)

    def beside(tasks):
        calls = iter(range(1000))

        def call():
            if next(calls) % 7 in (2, 4, 5) and tasks:
                tasks.pop(0)()

        return call

    tasks = [functools.partial(residual, 0, prior_0, rows) for rows in chunks]
    tasks += [functools.partial(residual, 1, prior_1, rows) for rows in chunks]
    later = {}

    def cross():
        later["cross"] = columns(8, 2) - dot(prior_1, prior_0, 1, 1)

    def block():
        later["block"] = symmetrized(columns(10, 2)) - dot(prior_1, prior_1, 1, 1)

    tasks.insert(0, cross)
    tasks.insert(0, block)
    raw_block = columns(3, 2)
    lead = slice(0, 64)
    inverse_0 = cholesky_inverse(
        symmetrized(raw_block[lead, lead]) - dot(prior_0[lead], prior_0[lead], 1, 1),
        lambda: symmetrized(raw_block) - dot(prior_0, prior_0, 1, 1),
        beside(tasks),
    )
    lead_pivots = dot(later["cross"][lead], inverse_0, 1, 1)

    def block_1():
        later["fresh"] = dot(later["cross"], inverse_0, 1, 1)
        return later["block"] - dot(later["fresh"], later["fresh"], 1, 1)

    tasks += [functools.partial(finish, 0, inverse_0, rows) for rows in chunks]
    tasks += [functools.partial(take, rows) for rows in chunks]
    inverse_1 = cholesky_inverse(later["block"][lead, lead] - dot(lead_pivots, lead_pivots, 1, 1), block_1, beside(tasks))
    for task in tasks:
        task()
    for rows in chunks:
        finish(1, inverse_1, rows)
    for copy in copies:
        copy.wait()


def steps(mine, other, prior, raw):
    vmem = pl.BlockSpec(memory_space=pltpu.VMEM)
    groups = mine.shape[0]
    return pl.pallas_call(
        steps_kernel,
        out_shape=jax.ShapeDtypeStruct(raw.shape, F32),
        in_specs=[vmem] * 4,
        out_specs=pl.BlockSpec(memory_space=pl.ANY),
        scratch_shapes=[
            pltpu.VMEM((2 * groups, 12) + TILE, F32),
            pltpu.VMEM(raw.shape, F32),
            pltpu.SemaphoreType.DMA((8,)),
        ],
        compiler_params=pltpu.CompilerParams(vmem_limit_bytes=VMEM_LIMIT),
    )(mine, other, prior, raw)


def body(prior, raw, pivot_rows):
    plane, line = ("y", "x"), ("z_hi", "z_lo")
    in_plane = lax.axis_size(plane)
    swap = [(0, 1), (1, 0)]

    keep, send = pack(pivot_rows, prior, raw, in_plane)
    total = keep + lax.ppermute(send, "core", swap)
    total = jnp.sum(lax.all_to_all(total, plane, 0, 0), axis=0)
    for groups in ([[4 * run + k for k in range(4)] for run in range(4)], [[4 * run + k for run in range(4)] for k in range(4)]):
        copies = jnp.broadcast_to(total, (4,) + total.shape)
        total = jnp.sum(lax.all_to_all(copies, line, 0, 0, axis_index_groups=groups), axis=0)
    mine = lax.all_to_all(jnp.broadcast_to(total, (in_plane,) + total.shape), plane, 0, 0)
    other = lax.ppermute(mine, "core", swap)
    return steps(mine, other, prior, raw)


def solution(mesh):
    fine = Mesh(mesh.devices.reshape(2, 4, 4, 2, 8), AXES)
    return jax.shard_map(
        body,
        mesh=fine,
        in_specs=(P(AXES, None), P(None, AXES, None), P()),
        out_specs=P(None, AXES, None),
        check_vma=False,
    )
```

```python
import functools

import jax
import jax.numpy as jnp
from jax import lax
from jax.experimental import pallas as pl
from jax.experimental.pallas import tpu as pltpu
from jax.sharding import Mesh
from jax.sharding import PartitionSpec as P

F32 = jnp.float32
HIGHEST = lax.Precision.HIGHEST
AXES = ("z_hi", "y", "x", "core", "z_lo")
TILE = (8, 128)
VMEM_LIMIT = 48 * 1024 * 1024
PACK_VMEM_LIMIT = 56 * 1024 * 1024


def dot(left, right, left_dim=1, right_dim=0):
    dims = (((left_dim,), (right_dim,)), ((), ()))
    return lax.dot_general(left, right, dims, precision=HIGHEST, preferred_element_type=F32)


def pack_kernel(pivots, prior, raw, keep, send, counts, sem):
    keep[...] = jnp.zeros_like(keep)
    send[...] = jnp.zeros_like(send)
    rows_here = prior.shape[0]
    offset, core = lax.axis_index(AXES) * rows_here, lax.axis_index("core")
    per_step = pivots.shape[1]
    chunk = 8

    def local(step, pivot):
        row = pivots[step, pivot] - offset
        return row, row.astype(jnp.uint32) < jnp.uint32(rows_here)

    def tiles(step):
        base = 5 * step
        for t in range(3):
            yield base + t, prior, 128 * t
        for which in range(step + 1):
            for t in range(2):
                yield base + 3 + 2 * which + t, raw.at[which], 128 * t

    def copy(source, row, column, target):
        return pltpu.make_async_copy(source.at[pl.ds(row, 1), pl.ds(column, 128)], target, sem)

    def start(step, pivot):
        row, here = local(step, pivot)

        @pl.when(here)
        def _():
            counts[step] += 1
            half = keep.shape[0]
            group, line = pivot // 8, pl.ds(lax.rem(pivot, 8), 1)
            for side, target in ((core, keep), (1 - core, send)):

                @pl.when(group // half == side)
                def _():
                    for number, source, column in tiles(step):
                        copy(source, row, column, target.at[lax.rem(group, half), number, line]).start()

    for step in range(2):
        counts[step] = 0

        for first in range(0, per_step, chunk):
            found = local(step, first)[1]
            for k in range(1, chunk):
                found = jnp.logical_or(found, local(step, first + k)[1])

            @pl.when(found)
            def _(step=step, first=first):
                lax.fori_loop(0, chunk, lambda k, _: start(step, first + k), None)

    for step in range(2):

        def finish(_, carry, step=step):
            for _, source, column in tiles(step):
                copy(source, 0, column, keep.at[0, 0, pl.ds(0, 1)]).wait()
            return carry

        lax.fori_loop(0, counts[step], finish, 0)


def pack(pivot_rows, prior, raw, groups):
    shape = pltpu.VMEM((groups, 12) + TILE, F32)
    vmem, smem = pl.BlockSpec(memory_space=pltpu.VMEM), pl.BlockSpec(memory_space=pltpu.SMEM)
    where_it_is = pl.BlockSpec(memory_space=pl.ANY)
    return pl.pallas_call(
        pack_kernel,
        out_shape=(shape, shape),
        in_specs=[smem, where_it_is, where_it_is],
        out_specs=(vmem, vmem),
        scratch_shapes=[pltpu.SMEM((2,), jnp.int32), pltpu.SemaphoreType.DMA],
        compiler_params=pltpu.CompilerParams(vmem_limit_bytes=PACK_VMEM_LIMIT),
    )(pivot_rows, prior, raw)


def spread(line):
    return jnp.broadcast_to(line, TILE)


def eliminate(block, at, beside):
    width = block.shape[0]
    row_of = lax.broadcasted_iota(jnp.int32, (width, width), 0)
    column_of = lax.broadcasted_iota(jnp.int32, (width, width), 1)
    line_of = lax.broadcasted_iota(jnp.int32, TILE, 0)
    halves = [block, (row_of == column_of).astype(F32)]
    work = jnp.concatenate(halves[:: -1 if at else 1], axis=1)
    done = []
    columns = [jnp.broadcast_to(work[:8, at + k : at + k + 1], TILE) for k in range(8)]
    for first in range(0, width, 8):
        left = width - first
        below = left // 8 - 1
        head, finished, rows, under, after = work[:8], work[:8], [], [], []
        if below:
            for k in range(8, 16):
                after.append(jnp.broadcast_to(work[8:16, at + first + k : at + first + k + 1], TILE))
            for k in range(8):
                column = jnp.broadcast_to(work[8:, at + first + k : at + first + k + 1], (left - 8, 128))
                under.append(column.reshape((below,) + TILE))
        for k in range(8):
            root = lax.rsqrt(spread(columns[k][k : k + 1]))
            scaled = columns[k] * root
            rows.append(spread(head[k : k + 1]) * root)
            finished = jnp.where(line_of == k, rows[k], finished)
            if k < 7:
                head = head - scaled * rows[k]
            if below:
                under[k] = under[k] * root
            for m in range(k + 1, 8):
                factor = spread(scaled[m : m + 1])
                columns[m] = columns[m] - scaled * factor
                if below:
                    under[m] = under[m] - under[k] * factor
        done.append(finished)
        if below:
            for k in range(8):
                column = under[k][0]
                for m in range(8):
                    after[m] = after[m] - column * spread(column[m : m + 1])
            columns = after
            work = work[8:].reshape((below,) + TILE)
            for k in range(8):
                work = work - under[k] * rows[k]
            work = work.reshape(left - 8, 128)
        beside()
    return jnp.concatenate(done, axis=0)


def cholesky_inverse(first, whole, beside):
    width, size = first.shape[0], 4 * first.shape[0]
    finished, made = [], []
    for which in range(size // width):
        low, high = which * width, (which + 1) * width
        at = low % 128
        rest = size - high
        urgent = [whole]

        def call(urgent=urgent):
            if urgent:
                made.append(urgent.pop()())
            else:
                beside()

        inverse = eliminate(first, at, call)
        work = made[-1]
        block_of = lax.broadcasted_iota(jnp.int32, (width, size), 1) // width
        on_diagonal = lax.broadcasted_iota(jnp.int32, (width, size), 1) == lax.broadcasted_iota(jnp.int32, (width, size), 0) + low
        line = jnp.where(block_of == which, on_diagonal.astype(F32), work[:width])
        blank = jnp.zeros_like(line)
        line = dot(inverse, jnp.concatenate([blank, line] if at == 0 else [line, blank], axis=0))
        if rest:
            column = work[width:, low:high]
            blank = jnp.zeros_like(column)
            column = jnp.concatenate([blank, column] if at == 0 else [column, blank], axis=1)
            tile = slice(high // 128 * 128, high // 128 * 128 + 128)
            near = work[width : 2 * width, tile] - dot(dot(column[:width], inverse, 1, 1), line[:, tile])
            first = near[:, high % 128 : high % 128 + width]

            def whole(work=work, column=column, inverse=inverse, line=line, which=which, rest=rest):
                block_of = lax.broadcasted_iota(jnp.int32, (rest, size), 1) // width
                return jnp.where(block_of == which, 0.0, work[width:]) - dot(dot(column, inverse, 1, 1), line)

        finished.append(jnp.where(block_of <= which, line, 0.0))
    return jnp.concatenate(finished, axis=0)


def steps_kernel(mine, other, prior, raw, result, packed, out, sems):
    core = lax.axis_index("core")
    half = mine.shape[0]
    packed[pl.ds(core * half, half)] = mine[...]
    packed[pl.ds((1 - core) * half, half)] = other[...]

    def columns(first, count):
        tiles = [packed[:, first + t].reshape(2 * half * 8, 128) for t in range(count)]
        return jnp.concatenate(tiles, axis=1)

    prior_0, prior_1 = columns(0, 3), columns(5, 3)
    rows_here = prior.shape[0]
    copies = []
    chunks = [slice(rows_here * c // 4, rows_here * (c + 1) // 4) for c in range(4)]

    def symmetrized(block):
        return 0.5 * (block + block.T)

    def residual(step, pivots, rows):
        out[step, rows] = raw[step, rows] - dot(prior[rows], pivots, 1, 1)

    def finish(step, inverse, rows):
        out[step, rows] = dot(out[step, rows], inverse, 1, 1)
        copies.append(pltpu.make_async_copy(out.at[step, rows], result.at[step, rows], sems.at[len(copies)]))
        copies[-1].start()

    def take(rows):
        out[1, rows] = out[1, rows] - dot(out[0, rows], later["fresh"], 1, 1)

    def beside(tasks):
        calls = iter(range(1000))

        def call():
            if next(calls) % 7 in (2, 4, 5) and tasks:
                tasks.pop(0)()

        return call

    tasks = [functools.partial(residual, 0, prior_0, rows) for rows in chunks]
    tasks += [functools.partial(residual, 1, prior_1, rows) for rows in chunks]
    later = {}

    def cross():
        later["cross"] = columns(8, 2) - dot(prior_1, prior_0, 1, 1)

    def block():
        later["block"] = symmetrized(columns(10, 2)) - dot(prior_1, prior_1, 1, 1)

    tasks.insert(0, cross)
    tasks.insert(0, block)
    raw_block = columns(3, 2)
    lead = slice(0, 64)
    inverse_0 = cholesky_inverse(
        symmetrized(raw_block[lead, lead]) - dot(prior_0[lead], prior_0[lead], 1, 1),
        lambda: symmetrized(raw_block) - dot(prior_0, prior_0, 1, 1),
        beside(tasks),
    )
    lead_pivots = dot(later["cross"][lead], inverse_0, 1, 1)

    def block_1():
        later["fresh"] = dot(later["cross"], inverse_0, 1, 1)
        return later["block"] - dot(later["fresh"], later["fresh"], 1, 1)

    tasks += [functools.partial(finish, 0, inverse_0, rows) for rows in chunks]
    tasks += [functools.partial(take, rows) for rows in chunks]
    inverse_1 = cholesky_inverse(later["block"][lead, lead] - dot(lead_pivots, lead_pivots, 1, 1), block_1, beside(tasks))
    for task in tasks:
        task()
    for rows in chunks:
        finish(1, inverse_1, rows)
    for copy in copies:
        copy.wait()


def steps(mine, other, prior, raw):
    vmem = pl.BlockSpec(memory_space=pltpu.VMEM)
    groups = mine.shape[0]
    return pl.pallas_call(
        steps_kernel,
        out_shape=jax.ShapeDtypeStruct(raw.shape, F32),
        in_specs=[vmem] * 4,
        out_specs=pl.BlockSpec(memory_space=pl.ANY),
        scratch_shapes=[
            pltpu.VMEM((2 * groups, 12) + TILE, F32),
            pltpu.VMEM(raw.shape, F32),
            pltpu.SemaphoreType.DMA((8,)),
        ],
        compiler_params=pltpu.CompilerParams(vmem_limit_bytes=VMEM_LIMIT),
    )(mine, other, prior, raw)


def body(prior, raw, pivot_rows):
    plane, line = ("y", "x"), ("z_hi", "z_lo")
    in_plane = lax.axis_size(plane)
    swap = [(0, 1), (1, 0)]

    keep, send = pack(pivot_rows, prior, raw, in_plane)
    total = keep + lax.ppermute(send, "core", swap)
    total = jnp.sum(lax.all_to_all(total, plane, 0, 0), axis=0)
    for groups in ([[4 * run + k for run in range(4)] for k in range(4)], [[4 * run + k for k in range(4)] for run in range(4)]):
        copies = jnp.broadcast_to(total, (4,) + total.shape)
        total = jnp.sum(lax.all_to_all(copies, line, 0, 0, axis_index_groups=groups), axis=0)
    mine = lax.all_to_all(jnp.broadcast_to(total, (in_plane,) + total.shape), plane, 0, 0)
    other = lax.ppermute(mine, "core", swap)
    return steps(mine, other, prior, raw)


def solution(mesh):
    fine = Mesh(mesh.devices.reshape(2, 4, 4, 2, 8), AXES)
    return jax.shard_map(
        body,
        mesh=fine,
        in_specs=(P(AXES, None), P(None, AXES, None), P()),
        out_specs=P(None, AXES, None),
        check_vma=False,
    )
```

```python
import functools

import jax
import jax.numpy as jnp
from jax import lax
from jax.experimental import pallas as pl
from jax.experimental.pallas import tpu as pltpu
from jax.sharding import Mesh
from jax.sharding import PartitionSpec as P

F32 = jnp.float32
HIGHEST = lax.Precision.HIGHEST
AXES = ("z_hi", "y", "x", "core", "z_lo")
TILE = (8, 128)
VMEM_LIMIT = 48 * 1024 * 1024
PACK_VMEM_LIMIT = 56 * 1024 * 1024


def dot(left, right, left_dim=1, right_dim=0):
    dims = (((left_dim,), (right_dim,)), ((), ()))
    return lax.dot_general(left, right, dims, precision=HIGHEST, preferred_element_type=F32)


def pack_kernel(own, pivots, prior, raw, packed, counts, sem):
    packed[...] = jnp.zeros_like(packed)
    rows_here = prior.shape[0]
    offset, core = lax.axis_index(AXES) * rows_here, lax.axis_index("core")
    half = packed.shape[0] * 8
    base = (core if own else 1 - core) * half
    chunk = 8

    def local(step, pivot):
        row = pivots[step, base + pivot] - offset
        return row, row.astype(jnp.uint32) < jnp.uint32(rows_here)

    def tiles(step):
        first = 5 * step
        for t in range(3):
            yield first + t, prior, 128 * t
        for which in range(step + 1):
            for t in range(2):
                yield first + 3 + 2 * which + t, raw.at[which], 128 * t

    def copy(source, row, column, target):
        return pltpu.make_async_copy(source.at[pl.ds(row, 1), pl.ds(column, 128)], target, sem)

    def start(step, group, line):
        row, here = local(step, 8 * group + line)

        @pl.when(here)
        def _():
            counts[step] += 1
            for number, source, column in tiles(step):
                copy(source, row, column, packed.at[group, number, pl.ds(line, 1)]).start()

    for step in range(2):
        counts[step] = 0
        for first in range(0, half, chunk):
            found = local(step, first)[1]
            for k in range(1, chunk):
                found = jnp.logical_or(found, local(step, first + k)[1])

            @pl.when(found)
            def _(step=step, first=first):
                lax.fori_loop(0, chunk, lambda k, _: start(step, first // 8, k), None)

    for step in range(2):

        def finish(_, carry, step=step):
            for _, source, column in tiles(step):
                copy(source, 0, column, packed.at[0, 0, pl.ds(0, 1)]).wait()
            return carry

        lax.fori_loop(0, counts[step], finish, 0)


def pack(own, pivot_rows, prior, raw, groups):
    vmem, smem = pl.BlockSpec(memory_space=pltpu.VMEM), pl.BlockSpec(memory_space=pltpu.SMEM)
    where_it_is = pl.BlockSpec(memory_space=pl.ANY)
    return pl.pallas_call(
        functools.partial(pack_kernel, own),
        out_shape=pltpu.VMEM((groups, 12) + TILE, F32),
        in_specs=[smem, where_it_is, where_it_is],
        out_specs=vmem,
        scratch_shapes=[pltpu.SMEM((2,), jnp.int32), pltpu.SemaphoreType.DMA],
        compiler_params=pltpu.CompilerParams(vmem_limit_bytes=PACK_VMEM_LIMIT),
        cost_estimate=pl.CostEstimate(flops=0, bytes_accessed=4 * 1024 * 1024, transcendentals=0),
    )(pivot_rows, prior, raw)


def spread(line):
    return jnp.broadcast_to(line, TILE)


def eliminate(block, at, beside):
    width = block.shape[0]
    row_of = lax.broadcasted_iota(jnp.int32, (width, width), 0)
    column_of = lax.broadcasted_iota(jnp.int32, (width, width), 1)
    line_of = lax.broadcasted_iota(jnp.int32, TILE, 0)
    halves = [block, (row_of == column_of).astype(F32)]
    work = jnp.concatenate(halves[:: -1 if at else 1], axis=1)
    done = []
    columns = [jnp.broadcast_to(work[:8, at + k : at + k + 1], TILE) for k in range(8)]
    for first in range(0, width, 8):
        left = width - first
        below = left // 8 - 1
        head, finished, rows, under, after = work[:8], work[:8], [], [], []
        if below:
            for k in range(8, 16):
                after.append(jnp.broadcast_to(work[8:16, at + first + k : at + first + k + 1], TILE))
            for k in range(8):
                column = jnp.broadcast_to(work[8:, at + first + k : at + first + k + 1], (left - 8, 128))
                under.append(column.reshape((below,) + TILE))
        for k in range(8):
            root = lax.rsqrt(spread(columns[k][k : k + 1]))
            scaled = columns[k] * root
            rows.append(spread(head[k : k + 1]) * root)
            finished = jnp.where(line_of == k, rows[k], finished)
            if k < 7:
                head = head - scaled * rows[k]
            if below:
                under[k] = under[k] * root
            for m in range(k + 1, 8):
                factor = spread(scaled[m : m + 1])
                columns[m] = columns[m] - scaled * factor
                if below:
                    under[m] = under[m] - under[k] * factor
        done.append(finished)
        if below:
            for k in range(8):
                column = under[k][0]
                for m in range(8):
                    after[m] = after[m] - column * spread(column[m : m + 1])
            columns = after
            work = work[8:].reshape((below,) + TILE)
            for k in range(8):
                work = work - under[k] * rows[k]
            work = work.reshape(left - 8, 128)
        beside()
    return jnp.concatenate(done, axis=0)


def cholesky_inverse(first, whole, beside):
    width, size = first.shape[0], 4 * first.shape[0]
    finished, made = [], []
    for which in range(size // width):
        low, high = which * width, (which + 1) * width
        at = low % 128
        rest = size - high
        urgent = [whole]

        def call(urgent=urgent):
            if urgent:
                made.append(urgent.pop()())
            else:
                beside()

        inverse = eliminate(first, at, call)
        work = made[-1]
        block_of = lax.broadcasted_iota(jnp.int32, (width, size), 1) // width
        on_diagonal = lax.broadcasted_iota(jnp.int32, (width, size), 1) == lax.broadcasted_iota(jnp.int32, (width, size), 0) + low
        line = jnp.where(block_of == which, on_diagonal.astype(F32), work[:width])
        blank = jnp.zeros_like(line)
        line = dot(inverse, jnp.concatenate([blank, line] if at == 0 else [line, blank], axis=0))
        if rest:
            column = work[width:, low:high]
            blank = jnp.zeros_like(column)
            column = jnp.concatenate([blank, column] if at == 0 else [column, blank], axis=1)
            tile = slice(high // 128 * 128, high // 128 * 128 + 128)
            near = work[width : 2 * width, tile] - dot(dot(column[:width], inverse, 1, 1), line[:, tile])
            first = near[:, high % 128 : high % 128 + width]

            def whole(work=work, column=column, inverse=inverse, line=line, which=which, rest=rest):
                block_of = lax.broadcasted_iota(jnp.int32, (rest, size), 1) // width
                return jnp.where(block_of == which, 0.0, work[width:]) - dot(dot(column, inverse, 1, 1), line)

        finished.append(jnp.where(block_of <= which, line, 0.0))
    return jnp.concatenate(finished, axis=0)


def steps_kernel(mine, other, prior, raw, result, packed, out, sems):
    core = lax.axis_index("core")
    half = mine.shape[0]
    packed[pl.ds(core * half, half)] = mine[...]
    packed[pl.ds((1 - core) * half, half)] = other[...]

    def columns(first, count):
        tiles = [packed[:, first + t].reshape(2 * half * 8, 128) for t in range(count)]
        return jnp.concatenate(tiles, axis=1)

    prior_0, prior_1 = columns(0, 3), columns(5, 3)
    rows_here = prior.shape[0]
    copies = []
    chunks = [slice(rows_here * c // 4, rows_here * (c + 1) // 4) for c in range(4)]

    def symmetrized(block):
        return 0.5 * (block + block.T)

    def residual(step, pivots, rows):
        out[step, rows] = raw[step, rows] - dot(prior[rows], pivots, 1, 1)

    def finish(step, inverse, rows):
        out[step, rows] = dot(out[step, rows], inverse, 1, 1)
        copies.append(pltpu.make_async_copy(out.at[step, rows], result.at[step, rows], sems.at[len(copies)]))
        copies[-1].start()

    def take(rows):
        out[1, rows] = out[1, rows] - dot(out[0, rows], later["fresh"], 1, 1)

    def beside(tasks):
        calls = iter(range(1000))

        def call():
            if next(calls) % 7 in (2, 4, 5) and tasks:
                tasks.pop(0)()

        return call

    tasks = [functools.partial(residual, 0, prior_0, rows) for rows in chunks]
    tasks += [functools.partial(residual, 1, prior_1, rows) for rows in chunks]
    later = {}

    def cross():
        later["cross"] = columns(8, 2) - dot(prior_1, prior_0, 1, 1)

    def block():
        later["block"] = symmetrized(columns(10, 2)) - dot(prior_1, prior_1, 1, 1)

    tasks.insert(0, cross)
    tasks.insert(0, block)
    raw_block = columns(3, 2)
    lead = slice(0, 64)
    inverse_0 = cholesky_inverse(
        symmetrized(raw_block[lead, lead]) - dot(prior_0[lead], prior_0[lead], 1, 1),
        lambda: symmetrized(raw_block) - dot(prior_0, prior_0, 1, 1),
        beside(tasks),
    )
    lead_pivots = dot(later["cross"][lead], inverse_0, 1, 1)

    def block_1():
        later["fresh"] = dot(later["cross"], inverse_0, 1, 1)
        return later["block"] - dot(later["fresh"], later["fresh"], 1, 1)

    tasks += [functools.partial(finish, 0, inverse_0, rows) for rows in chunks]
    tasks += [functools.partial(take, rows) for rows in chunks]
    inverse_1 = cholesky_inverse(later["block"][lead, lead] - dot(lead_pivots, lead_pivots, 1, 1), block_1, beside(tasks))
    for task in tasks:
        task()
    for rows in chunks:
        finish(1, inverse_1, rows)
    for copy in copies:
        copy.wait()


def steps(mine, other, prior, raw):
    vmem = pl.BlockSpec(memory_space=pltpu.VMEM)
    groups = mine.shape[0]
    return pl.pallas_call(
        steps_kernel,
        out_shape=jax.ShapeDtypeStruct(raw.shape, F32),
        in_specs=[vmem] * 4,
        out_specs=pl.BlockSpec(memory_space=pl.ANY),
        scratch_shapes=[
            pltpu.VMEM((2 * groups, 12) + TILE, F32),
            pltpu.VMEM(raw.shape, F32),
            pltpu.SemaphoreType.DMA((8,)),
        ],
        compiler_params=pltpu.CompilerParams(vmem_limit_bytes=VMEM_LIMIT),
    )(mine, other, prior, raw)


def body(prior, raw, pivot_rows):
    plane, line = ("y", "x"), ("z_hi", "z_lo")
    in_plane = lax.axis_size(plane)
    swap = [(0, 1), (1, 0)]

    came = lax.ppermute(pack(False, pivot_rows, prior, raw, in_plane), "core", swap)
    total = pack(True, pivot_rows, prior, raw, in_plane) + came
    total = jnp.sum(lax.all_to_all(total, plane, 0, 0), axis=0)
    for groups in ([[4 * run + k for k in range(4)] for run in range(4)], [[4 * run + k for run in range(4)] for k in range(4)]):
        copies = jnp.broadcast_to(total, (4,) + total.shape)
        total = jnp.sum(lax.all_to_all(copies, line, 0, 0, axis_index_groups=groups), axis=0)
    mine = lax.all_to_all(jnp.broadcast_to(total, (in_plane,) + total.shape), plane, 0, 0)
    other = lax.ppermute(mine, "core", swap)
    return steps(mine, other, prior, raw)


def solution(mesh):
    fine = Mesh(mesh.devices.reshape(2, 4, 4, 2, 8), AXES)
    return jax.shard_map(
        body,
        mesh=fine,
        in_specs=(P(AXES, None), P(None, AXES, None), P()),
        out_specs=P(None, AXES, None),
        check_vma=False,
    )
```
